32 devices in a mesh: grp: 2 (over x), cell: 16 (over z, y, core).
Axes of the slice: x: 2, y: 2, z: 4, core: 2. Of those that a mesh axis runs over, the one named last changes fastest.
Arguments:
- fields: bfloat16 [8192, 3, 8192], P(('grp', 'cell')), parts along dimension 0, may hold values from -6 to 6
- horiz: float32 [16384], P(('grp', 'cell')), parts along dimension 0, may hold values from 0.2 to 1
- vertical: float32 [16384], P(('grp', 'cell')), parts along dimension 0, may hold values from 1.5 to 6
- tilt_angle: float32 [16384], P(('grp', 'cell')), parts along dimension 0, may hold values from 0.2 to 1.4
- azimuth: float32 [16384], P(('grp', 'cell')), parts along dimension 0, may hold values from -3.140625 to 3.140625
- electrode_quads: int32 [4096, 4], P('grp'), parts along dimension 0, may hold values from 0 to 4095, as said below
Outputs:
- jacobian: bfloat16 [4096, 4, 8192], P('grp', None, 'cell'), parts along dimension 0
- coverage: float32 [16384], P(('grp', 'cell')), parts along dimension 0
The draws below stay inside these ranges and needn't reach their ends.
There are 2 independent parts, one for each index of `grp`. The reference program is written for one: setup_inputs(seed, part) draws one part's arguments, and reference() takes and returns one part's arrays. A program takes and returns all parts, laid end to end along the dimension named above; each array names one. Nothing has to cross between parts.
Inputs may be any that keep to these rules, and one draw needn't show every extreme that they name: `electrode_quads`: each row names four different electrodes.
All inputs are finite; a program needn't handle non-finite values.
Results may differ from the reference program's by a relative error of at most 0.001.
Values may be sent and summed in bfloat16 or wider, within the bound.
A program may use at most 192 MiB of HBM per device.

```python
import math
import jax
import jax.numpy as jnp
from jax import lax

ELECTRODE_COUNT = 4096
QUAD_READINGS = 2048
CELL_TOTAL = 8192


def draw_electrode_quads(key, part):
    random_keys = jax.random.split(key, 4)
    base_offset = jax.random.randint(random_keys[0], (QUAD_READINGS,), 0, ELECTRODE_COUNT)
    base_offset = base_offset.at[0].set(ELECTRODE_COUNT - 1).at[1].set(0)
    quarter_size = ELECTRODE_COUNT // 4
    first_quarter = jax.random.randint(random_keys[1], (QUAD_READINGS,), 1, quarter_size)
    second_quarter = jax.random.randint(random_keys[2], (QUAD_READINGS,), quarter_size, 2 * quarter_size)
    third_quarter = jax.random.randint(random_keys[3], (QUAD_READINGS,), 2 * quarter_size, 3 * quarter_size)
    return jnp.stack([base_offset, (base_offset + first_quarter) % ELECTRODE_COUNT, (base_offset + second_quarter) % ELECTRODE_COUNT, (base_offset + third_quarter) % ELECTRODE_COUNT], axis=1).astype(jnp.int32)


def block_scale(own_key, dims, cuts, low, top_value):
    def one(dim, blocks):
        steps = jax.random.uniform(jax.random.fold_in(jax.random.fold_in(own_key, 6), dim), (blocks,), jnp.float32, low / len(cuts), top_value / len(cuts))
        return jnp.repeat(jnp.exp(steps), dims[dim] // blocks).reshape((-1,) + (1,) * (len(dims) - dim - 1))

    level = one(*cuts[0])
    for cut in cuts[1:]:
        level = level * one(*cut)
    return level


def gaussian(rng, extent, width, most, cuts=(), held_as=jnp.bfloat16):
    drawn = width * jax.random.normal(rng, extent, jnp.float32)
    if cuts:
        drawn = drawn * block_scale(rng, extent, cuts, -0.22, 0.18)
    return jnp.clip(drawn, -most, most).astype(held_as)


def setup_inputs(seed: int = 0, part: int = 0) -> dict:
    streams_of = jax.random.split(jax.random.key(seed), 7)
    part_keys = jax.random.split(jax.random.fold_in(streams_of[6], part), 7)
    fields = gaussian(part_keys[0], (ELECTRODE_COUNT, 3, CELL_TOTAL), 1.0, 6.0, ((0, 16),))
    horiz = jnp.clip(jnp.exp(math.log(1.0) - 1.609438 * jax.random.uniform(part_keys[1], (CELL_TOTAL,), jnp.float32) ** block_scale(part_keys[1], (CELL_TOTAL,), ((0, 16),), -0.2, 0.2)), 0.2, 1.0)
    vertical = jnp.clip(jnp.exp(math.log(6.0) - 1.3862944 * jax.random.uniform(part_keys[2], (CELL_TOTAL,), jnp.float32) ** block_scale(part_keys[2], (CELL_TOTAL,), ((0, 16),), -0.2, 0.2)), 1.5, 6.0)
    tilt_angle = jnp.clip(0.2 + 1.19999997 * jax.random.uniform(part_keys[3], (CELL_TOTAL,), jnp.float32) ** block_scale(part_keys[3], (CELL_TOTAL,), ((0, 16),), -0.2, 0.2), 0.2, 1.4)
    azimuth = jnp.clip(jax.random.uniform(part_keys[4], (CELL_TOTAL,), jnp.float32, -3.140625, 3.140625), -3.140625, 3.140625)
    electrode_quads = draw_electrode_quads(jax.random.fold_in(jax.random.fold_in(streams_of[6], part), 71), part)
    return {"fields": fields, "horiz": horiz, "vertical": vertical, "tilt_angle": tilt_angle, "azimuth": azimuth, "electrode_quads": electrode_quads}


def sensitivity(grads, horiz, vertical, tilt_angle, azimuth, rows):

    def pick(column):
        return jnp.take(grads, rows[:, column], axis=0).astype(jnp.float32)
    source = pick(0) - pick(1)
    receiver = pick(2) - pick(3)
    sin_t = jnp.sin(tilt_angle)
    cos_t = jnp.cos(tilt_angle)
    sin_p = jnp.sin(azimuth)
    cos_p = jnp.cos(azimuth)
    axis_dir = jnp.stack([sin_t * cos_p, sin_t * sin_p, cos_t])
    tilt_dir = jnp.stack([cos_t * cos_p, cos_t * sin_p, -sin_t])
    turn_dir = jnp.stack([-sin_t * sin_p, sin_t * cos_p, jnp.zeros_like(sin_t)])

    def along(field, direction):
        return lax.optimization_barrier(jnp.sum(field * direction[None], axis=1))
    s_axis = along(source, axis_dir)
    r_axis = along(receiver, axis_dir)
    s_tilt = along(source, tilt_dir)
    r_tilt = along(receiver, tilt_dir)
    s_turn = along(source, turn_dir)
    r_turn = along(receiver, turn_dir)
    inner = lax.optimization_barrier(jnp.sum(source * receiver, axis=1))
    contrast = vertical - horiz
    return jnp.stack([-horiz * (inner - s_axis * r_axis), -vertical * s_axis * r_axis, -contrast * (s_tilt * r_axis + s_axis * r_tilt), -contrast * (s_turn * r_axis + s_axis * r_turn)], axis=1)

def reference(fields, horiz, vertical, tilt_angle, azimuth, electrode_quads):
    block_slice = min(128, QUAD_READINGS)
    block_count = QUAD_READINGS // block_slice

    def one_block(rows):
        values = sensitivity(fields, horiz, vertical, tilt_angle, azimuth, rows)
        meansq = lax.optimization_barrier(jnp.sum(values * values, axis=(1, 2))) / (4.0 * CELL_TOTAL)
        normed = values * lax.rsqrt(meansq + 1e-06)[:, None, None]
        return (normed.astype(jnp.bfloat16), lax.optimization_barrier(jnp.sum(normed * normed, axis=(0, 1))))
    jacobian_blocks, coverage_blocks = lax.map(one_block, electrode_quads.reshape(block_count, block_slice, 4))
    return (jacobian_blocks.reshape(QUAD_READINGS, 4, CELL_TOTAL), lax.optimization_barrier(jnp.sum(coverage_blocks, axis=0)))
```

```python
import functools

import jax
import jax.numpy as jnp
from jax import lax
from jax.experimental import pallas as pl
from jax.experimental.pallas import tpu as pltpu
from jax.sharding import PartitionSpec as P

MESH = pl.DeviceIdType.MESH
LANES = 128


def greet(n, me):
    barrier = pltpu.get_barrier_semaphore()

    @pl.loop(1, n)
    def _(step):
        pl.semaphore_signal(barrier, inc=1, device_id={"cell": lax.rem(me + step, n)}, device_id_type=MESH)

    pl.semaphore_wait(barrier, n - 1)


def exchange_kernel(n, fields, gathered, send_sem, recv_sem, own_sem):
    me = lax.axis_index("cell")
    rows = fields.shape[1]
    cells = gathered.shape[2]
    greet(n, me)

    def landing(step):
        return gathered.at[:, pl.ds(pl.multiple_of(me * rows, rows), rows), :]

    def leaving(device):
        return fields.at[:, :, pl.ds(pl.multiple_of(device * cells, cells), cells)]

    def copy(step):
        peer = lax.rem(me + step, n)
        return pltpu.make_async_remote_copy(
            src_ref=leaving(peer),
            dst_ref=landing(step),
            send_sem=send_sem.at[step],
            recv_sem=recv_sem.at[step],
            device_id={"cell": peer},
            device_id_type=MESH,
        )

    @pl.loop(1, n)
    def _(step):
        copy(step).start()

    own = pltpu.make_async_copy(leaving(me), landing(0), own_sem)
    own.start()
    own.wait()

    @pl.loop(1, n)
    def _(step):
        copy(step).wait()


def exchange(fields, n, cells):
    comps, rows, _ = fields.shape
    return pl.pallas_call(
        functools.partial(exchange_kernel, n),
        out_shape=jax.ShapeDtypeStruct((comps, rows * n, cells), fields.dtype),
        in_specs=[pl.BlockSpec(memory_space=pl.ANY)],
        out_specs=pl.BlockSpec(memory_space=pl.ANY),
        scratch_shapes=[
            pltpu.SemaphoreType.DMA((n,)),
            pltpu.SemaphoreType.DMA((n,)),
            pltpu.SemaphoreType.DMA,
        ],
        compiler_params=pltpu.CompilerParams(collective_id=0, has_side_effects=True),
        name="exchange",
    )(fields)


def total_kernel(n, part, total, slots, send_sem, recv_sem):
    me = lax.axis_index("cell")
    greet(n, me)

    def copy(step):
        return pltpu.make_async_remote_copy(
            src_ref=part,
            dst_ref=slots.at[step],
            send_sem=send_sem.at[step],
            recv_sem=recv_sem.at[step],
            device_id={"cell": lax.rem(me + step, n)},
            device_id_type=MESH,
        )

    @pl.loop(1, n)
    def _(step):
        copy(step).start()

    slots[0] = part[...]

    @pl.loop(1, n)
    def _(step):
        copy(step).wait()

    total[...] = jnp.sum(slots[...], axis=0)


def total_of(part, n):
    return pl.pallas_call(
        functools.partial(total_kernel, n),
        out_shape=jax.ShapeDtypeStruct(part.shape, part.dtype),
        in_specs=[pl.BlockSpec(memory_space=pltpu.VMEM)],
        out_specs=pl.BlockSpec(memory_space=pltpu.VMEM),
        scratch_shapes=[
            pltpu.VMEM((n, *part.shape), part.dtype),
            pltpu.SemaphoreType.DMA((n,)),
            pltpu.SemaphoreType.DMA((n,)),
        ],
        compiler_params=pltpu.CompilerParams(collective_id=1, has_side_effects=True),
        name="total",
    )(part)


def sens_kernel(quads, grads, coef, sens, squares, wide, diffs):
    comps, electrodes, _ = grads.shape
    readings = squares.shape[0]
    chunk = pl.program_id(0)
    block = 256

    for c in range(comps):

        @pl.loop(0, electrodes // block)
        def _(i):
            at = pl.multiple_of(i * block, block)
            wide[pl.ds(c * electrodes + at, block), :] = grads[c, pl.ds(at, block), :].astype(jnp.float32)

    @pl.loop(0, readings // 8)
    def _(g):
        for u in range(8):
            q = g * 8 + u
            a, b, m, n = (quads[4 * q + j] for j in range(4))
            for c in range(comps):
                base = c * electrodes
                diffs[c, pl.ds(q, 1), :] = wide[pl.ds(base + a, 1), :] - wide[pl.ds(base + b, 1), :]
                diffs[comps + c, pl.ds(q, 1), :] = wide[pl.ds(base + m, 1), :] - wide[pl.ds(base + n, 1), :]

    tile = 16

    @pl.loop(0, readings // tile)
    def _(i):
        at = pl.multiple_of(i * tile, tile)
        s = [diffs[c, pl.ds(at, tile), :] for c in range(3)]
        r = [diffs[3 + c, pl.ds(at, tile), :] for c in range(3)]
        terms = [s[c] * r[c] for c in range(3)]
        terms += [s[i] * r[j] + s[j] * r[i] for i, j in ((0, 1), (0, 2), (1, 2))]
        square = None
        for p in range(4):
            value = terms[0] * coef[pl.ds(6 * p, 1), :]
            for k in range(1, 6):
                value = value + terms[k] * coef[pl.ds(6 * p + k, 1), :]
            sens[pl.ds(4 * at + p, tile, stride=4), :] = value
            square = value * value if square is None else square + value * value

        @pl.when(chunk == 0)
        def _():
            squares[pl.ds(at, tile), :] = square

        @pl.when(chunk > 0)
        def _():
            squares[pl.ds(at, tile), :] += square


def sensitivities(quads, gathered, coef):
    comps, electrodes, cells = gathered.shape
    readings = quads.shape[0] // 4
    return pl.pallas_call(
        sens_kernel,
        grid_spec=pltpu.PrefetchScalarGridSpec(
            num_scalar_prefetch=1,
            grid=(cells // LANES,),
            in_specs=[
                pl.BlockSpec((comps, electrodes, LANES), lambda k, _: (0, 0, k)),
                pl.BlockSpec((coef.shape[0], LANES), lambda k, _: (0, k)),
            ],
            out_specs=[
                pl.BlockSpec((readings * 4, LANES), lambda k, _: (0, k)),
                pl.BlockSpec((readings, LANES), lambda k, _: (0, 0)),
            ],
            scratch_shapes=[
                pltpu.VMEM((comps * electrodes, LANES), jnp.float32),
                pltpu.VMEM((2 * comps, readings, LANES), jnp.float32),
            ],
        ),
        out_shape=[
            jax.ShapeDtypeStruct((readings * 4, cells), jnp.float32),
            jax.ShapeDtypeStruct((readings, LANES), jnp.float32),
        ],
        compiler_params=pltpu.CompilerParams(vmem_limit_bytes=56 * 2**20),
        name="sens",
    )(quads, gathered, coef)


def norm_kernel(sens, scale, jacobian, coverage):
    count = sens.shape[0]

    @pl.when(pl.program_id(0) == 0)
    def _():
        coverage[...] = jnp.zeros_like(coverage)

    for lane in range(sens.shape[1] // LANES):
        at = pl.ds(lane * LANES, LANES)
        normed = sens[:, at] * scale[...]
        jacobian[:, :, at] = normed.reshape(count // 4, 4, LANES).astype(jnp.bfloat16)
        coverage[:, at] += jnp.sum((normed * normed).reshape(count // 8, 8, LANES), axis=0)


def normalise(sens, scale):
    rows, cells = sens.shape
    block = 1024
    return pl.pallas_call(
        norm_kernel,
        grid=(rows // block,),
        in_specs=[
            pl.BlockSpec((block, cells), lambda i: (i, 0)),
            pl.BlockSpec((block, LANES), lambda i: (i, 0)),
        ],
        out_specs=[
            pl.BlockSpec((block // 4, 4, cells), lambda i: (i, 0, 0)),
            pl.BlockSpec((8, cells), lambda i: (0, 0)),
        ],
        out_shape=[
            jax.ShapeDtypeStruct((rows // 4, 4, cells), jnp.bfloat16),
            jax.ShapeDtypeStruct((8, cells), jnp.float32),
        ],
        compiler_params=pltpu.CompilerParams(vmem_limit_bytes=48 * 2**20),
        name="norm",
    )(sens, scale)


def coefficients(horiz, vertical, tilt_angle, azimuth):
    sin_t, cos_t = jnp.sin(tilt_angle), jnp.cos(tilt_angle)
    sin_p, cos_p = jnp.sin(azimuth), jnp.cos(azimuth)
    axis = (sin_t * cos_p, sin_t * sin_p, cos_t)
    tilt = (cos_t * cos_p, cos_t * sin_p, -sin_t)
    turn = (-sin_t * sin_p, sin_t * cos_p, jnp.zeros_like(sin_t))
    contrast = vertical - horiz
    pairs = ((0, 0), (1, 1), (2, 2), (0, 1), (0, 2), (1, 2))
    rows = [-horiz * ((1.0 if i == j else 0.0) - axis[i] * axis[j]) for i, j in pairs]
    rows += [-vertical * axis[i] * axis[j] for i, j in pairs]
    for other in (tilt, turn):
        rows += [-contrast * (other[i] * axis[j] + axis[i] * other[j]) for i, j in pairs]
    return jnp.stack(rows)


def local(fields, horiz, vertical, tilt_angle, azimuth, electrode_quads):
    shards = lax.axis_size("cell")
    cells = horiz.shape[0]
    readings = electrode_quads.shape[0]
    gathered = exchange(fields.transpose(1, 0, 2), shards, cells)
    coef = coefficients(horiz, vertical, tilt_angle, azimuth)
    sens, squares = sensitivities(electrode_quads.reshape(-1), gathered, coef)
    part = jnp.sum(squares, axis=1).reshape(readings // LANES, LANES)
    meansq = total_of(part, shards).reshape(-1) / (4.0 * cells * shards)
    scale = jnp.broadcast_to(lax.rsqrt(meansq + 1e-06)[:, None, None], (readings, 4, LANES))
    jacobian, coverage = normalise(sens, scale.reshape(readings * 4, LANES))
    return jacobian, jnp.sum(coverage, axis=0)


def solution(mesh):
    placed = (
        P(("grp", "cell"), None, None),
        P(("grp", "cell")),
        P(("grp", "cell")),
        P(("grp", "cell")),
        P(("grp", "cell")),
        P("grp", None),
    )
    return jax.shard_map(
        local,
        mesh=mesh,
        in_specs=placed,
        out_specs=(P("grp", None, "cell"), P(("grp", "cell"))),
        check_vma=False,
    )
```

```python
import functools

import jax
import jax.numpy as jnp
from jax import lax
from jax.experimental import pallas as pl
from jax.experimental.pallas import tpu as pltpu
from jax.sharding import PartitionSpec as P

MESH = pl.DeviceIdType.MESH
LANES = 128


def greet(n, me):
    barrier = pltpu.get_barrier_semaphore()

    @pl.loop(1, n)
    def _(step):
        pl.semaphore_signal(barrier, inc=1, device_id={"cell": lax.rem(me + step, n)}, device_id_type=MESH)

    pl.semaphore_wait(barrier, n - 1)


def chunk_sensitivities(quads, grads, coef, sens, squares, wide, diffs):
    comps, electrodes, _ = wide.shape
    readings = squares.shape[0]
    block = 256

    @pl.loop(0, electrodes // block)
    def _(i):
        at = pl.multiple_of(i * block, block)
        for c in range(comps):
            wide[c, pl.ds(at, block), :] = grads[c, pl.ds(at, block), :].astype(jnp.float32)

    @pl.loop(0, readings // 8)
    def _(g):
        for u in range(8):
            q = g * 8 + u
            a, b, m, n = (quads[4 * q + j] for j in range(4))
            for c in range(comps):
                diffs[c, pl.ds(q, 1), :] = wide[c, pl.ds(a, 1), :] - wide[c, pl.ds(b, 1), :]
                diffs[comps + c, pl.ds(q, 1), :] = wide[c, pl.ds(m, 1), :] - wide[c, pl.ds(n, 1), :]

    tile = 16

    @pl.loop(0, readings // tile)
    def _(i):
        at = pl.multiple_of(i * tile, tile)
        s = [diffs[c, pl.ds(at, tile), :] for c in range(3)]
        r = [diffs[3 + c, pl.ds(at, tile), :] for c in range(3)]
        terms = [s[c] * r[c] for c in range(3)]
        terms += [s[i] * r[j] + s[j] * r[i] for i, j in ((0, 1), (0, 2), (1, 2))]
        square = squares[pl.ds(at, tile), :]
        for p in range(4):
            value = terms[0] * coef[pl.ds(6 * p, 1), :]
            for k in range(1, 6):
                value = value + terms[k] * coef[pl.ds(6 * p + k, 1), :]
            sens[pl.ds(4 * at + p, tile, stride=4), :] = value
            square = square + value * value
        squares[pl.ds(at, tile), :] = square


def exchange_kernel(
    n, quads, fields, coef, sens, squares, landed, ready, wide, diffs, send_sem, recv_sem, own_sem, out_sem
):
    me = lax.axis_index("cell")
    rows = fields.shape[1]
    chunks = landed.shape[0]
    cells = chunks * LANES
    greet(n, me)

    def landing(chunk):
        return landed.at[chunk, :, pl.ds(pl.multiple_of(me * rows, rows), rows), :]

    def leaving(device, chunk):
        return fields.at[:, :, pl.ds(pl.multiple_of(device * cells + chunk * LANES, LANES), LANES)]

    def copy(chunk, step):
        peer = lax.rem(me + step, n)
        return pltpu.make_async_remote_copy(
            src_ref=leaving(peer, chunk),
            dst_ref=landing(chunk),
            send_sem=send_sem.at[chunk, step],
            recv_sem=recv_sem.at[chunk, step],
            device_id={"cell": peer},
            device_id_type=MESH,
        )

    def own(chunk):
        return pltpu.make_async_copy(leaving(me, chunk), landing(chunk), own_sem.at[chunk])

    def out(chunk):
        at = pl.ds(pl.multiple_of(chunk * LANES, LANES), LANES)
        return pltpu.make_async_copy(ready.at[chunk], sens.at[:, at], out_sem.at[chunk])

    @pl.loop(0, chunks)
    def _(chunk):
        own(chunk).start()

        @pl.loop(1, n)
        def _(step):
            copy(chunk, step).start()

    squares[...] = jnp.zeros_like(squares)

    @pl.loop(0, chunks)
    def _(chunk):
        own(chunk).wait()

        @pl.loop(1, n)
        def _(step):
            copy(chunk, step).wait()

        chunk_sensitivities(
            quads, landed.at[chunk], coef.at[chunk], ready.at[chunk], squares, wide, diffs
        )
        out(chunk).start()

    @pl.loop(0, chunks)
    def _(chunk):
        out(chunk).wait()


def sensitivities(fields, quads, coef, n):
    comps, rows, _ = fields.shape
    chunks = coef.shape[0]
    electrodes, readings, cells = rows * n, quads.shape[0] // 4, chunks * LANES
    in_vmem = pl.BlockSpec(memory_space=pltpu.VMEM)
    anywhere = pl.BlockSpec(memory_space=pl.ANY)
    return pl.pallas_call(
        functools.partial(exchange_kernel, n),
        out_shape=[
            jax.ShapeDtypeStruct((readings * 4, cells), jnp.float32),
            jax.ShapeDtypeStruct((readings, LANES), jnp.float32),
        ],
        in_specs=[pl.BlockSpec(memory_space=pltpu.SMEM), anywhere, in_vmem],
        out_specs=[anywhere, in_vmem],
        scratch_shapes=[
            pltpu.VMEM((chunks, comps, electrodes, LANES), fields.dtype),
            pltpu.VMEM((chunks, readings * 4, LANES), jnp.float32),
            pltpu.VMEM((comps, electrodes, LANES), jnp.float32),
            pltpu.VMEM((2 * comps, readings, LANES), jnp.float32),
            pltpu.SemaphoreType.DMA((chunks, n)),
            pltpu.SemaphoreType.DMA((chunks, n)),
            pltpu.SemaphoreType.DMA((chunks,)),
            pltpu.SemaphoreType.DMA((chunks,)),
        ],
        compiler_params=pltpu.CompilerParams(
            collective_id=0, has_side_effects=True, vmem_limit_bytes=56 * 2**20
        ),
        name="exchange",
    )(quads, fields, coef)


def total_kernel(n, part, total, slots, send_sem, recv_sem):
    me = lax.axis_index("cell")
    greet(n, me)

    def copy(step):
        return pltpu.make_async_remote_copy(
            src_ref=part,
            dst_ref=slots.at[step],
            send_sem=send_sem.at[step],
            recv_sem=recv_sem.at[step],
            device_id={"cell": lax.rem(me + step, n)},
            device_id_type=MESH,
        )

    @pl.loop(1, n)
    def _(step):
        copy(step).start()

    slots[0] = part[...]

    @pl.loop(1, n)
    def _(step):
        copy(step).wait()

    total[...] = jnp.sum(slots[...], axis=0)


def total_of(part, n):
    return pl.pallas_call(
        functools.partial(total_kernel, n),
        out_shape=jax.ShapeDtypeStruct(part.shape, part.dtype),
        in_specs=[pl.BlockSpec(memory_space=pltpu.VMEM)],
        out_specs=pl.BlockSpec(memory_space=pltpu.VMEM),
        scratch_shapes=[
            pltpu.VMEM((n, *part.shape), part.dtype),
            pltpu.SemaphoreType.DMA((n,)),
            pltpu.SemaphoreType.DMA((n,)),
        ],
        compiler_params=pltpu.CompilerParams(collective_id=1, has_side_effects=True),
        name="total",
    )(part)


def norm_kernel(sens, scale, jacobian, coverage):
    count = sens.shape[0]

    @pl.when(pl.program_id(0) == 0)
    def _():
        coverage[...] = jnp.zeros_like(coverage)

    for lane in range(sens.shape[1] // LANES):
        at = pl.ds(lane * LANES, LANES)
        normed = sens[:, at] * scale[...]
        jacobian[:, :, at] = normed.reshape(count // 4, 4, LANES).astype(jnp.bfloat16)
        coverage[:, at] += jnp.sum((normed * normed).reshape(count // 8, 8, LANES), axis=0)


def normalise(sens, scale):
    rows, cells = sens.shape
    block = 1024
    return pl.pallas_call(
        norm_kernel,
        grid=(rows // block,),
        in_specs=[
            pl.BlockSpec((block, cells), lambda i: (i, 0)),
            pl.BlockSpec((block, LANES), lambda i: (i, 0)),
        ],
        out_specs=[
            pl.BlockSpec((block // 4, 4, cells), lambda i: (i, 0, 0)),
            pl.BlockSpec((8, cells), lambda i: (0, 0)),
        ],
        out_shape=[
            jax.ShapeDtypeStruct((rows // 4, 4, cells), jnp.bfloat16),
            jax.ShapeDtypeStruct((8, cells), jnp.float32),
        ],
        compiler_params=pltpu.CompilerParams(vmem_limit_bytes=48 * 2**20),
        name="norm",
    )(sens, scale)


def coefficients(horiz, vertical, tilt_angle, azimuth):
    sin_t, cos_t = jnp.sin(tilt_angle), jnp.cos(tilt_angle)
    sin_p, cos_p = jnp.sin(azimuth), jnp.cos(azimuth)
    axis = (sin_t * cos_p, sin_t * sin_p, cos_t)
    tilt = (cos_t * cos_p, cos_t * sin_p, -sin_t)
    turn = (-sin_t * sin_p, sin_t * cos_p, jnp.zeros_like(sin_t))
    contrast = vertical - horiz
    pairs = ((0, 0), (1, 1), (2, 2), (0, 1), (0, 2), (1, 2))
    rows = [-horiz * ((1.0 if i == j else 0.0) - axis[i] * axis[j]) for i, j in pairs]
    rows += [-vertical * axis[i] * axis[j] for i, j in pairs]
    for other in (tilt, turn):
        rows += [-contrast * (other[i] * axis[j] + axis[i] * other[j]) for i, j in pairs]
    return jnp.stack(rows)


def local(fields, horiz, vertical, tilt_angle, azimuth, electrode_quads):
    shards = lax.axis_size("cell")
    cells = horiz.shape[0]
    readings = electrode_quads.shape[0]
    coef = coefficients(horiz, vertical, tilt_angle, azimuth)
    coef = coef.reshape(coef.shape[0], cells // LANES, LANES).transpose(1, 0, 2)
    sens, squares = sensitivities(fields.transpose(1, 0, 2), electrode_quads.reshape(-1), coef, shards)
    part = jnp.sum(squares, axis=1).reshape(readings // LANES, LANES)
    meansq = total_of(part, shards).reshape(-1) / (4.0 * cells * shards)
    scale = jnp.broadcast_to(lax.rsqrt(meansq + 1e-06)[:, None, None], (readings, 4, LANES))
    jacobian, coverage = normalise(sens, scale.reshape(readings * 4, LANES))
    return jacobian, jnp.sum(coverage, axis=0)


def solution(mesh):
    placed = (
        P(("grp", "cell"), None, None),
        P(("grp", "cell")),
        P(("grp", "cell")),
        P(("grp", "cell")),
        P(("grp", "cell")),
        P("grp", None),
    )
    return jax.shard_map(
        local,
        mesh=mesh,
        in_specs=placed,
        out_specs=(P("grp", None, "cell"), P(("grp", "cell"))),
        check_vma=False,
    )
```

```python
import functools

import jax
import jax.numpy as jnp
from jax import lax
from jax.experimental import pallas as pl
from jax.experimental.pallas import tpu as pltpu
from jax.sharding import PartitionSpec as P

MESH = pl.DeviceIdType.MESH
LANES = 128


def greet(n, me):
    barrier = pltpu.get_barrier_semaphore()

    @pl.loop(1, n)
    def _(step):
        pl.semaphore_signal(barrier, inc=1, device_id={"cell": lax.rem(me + step, n)}, device_id_type=MESH)

    pl.semaphore_wait(barrier, n - 1)


def fill_coefficients(coef, horiz, vertical, sin_t, cos_t, sin_p, cos_p):
    axis = (sin_t * cos_p, sin_t * sin_p, cos_t)
    tilt = (cos_t * cos_p, cos_t * sin_p, -sin_t)
    turn = (-sin_t * sin_p, sin_t * cos_p, jnp.zeros_like(sin_t))
    contrast = vertical - horiz
    pairs = ((0, 0), (1, 1), (2, 2), (0, 1), (0, 2), (1, 2))
    rows = [-horiz * ((1.0 if i == j else 0.0) - axis[i] * axis[j]) for i, j in pairs]
    rows += [-vertical * axis[i] * axis[j] for i, j in pairs]
    for other in (tilt, turn):
        rows += [-contrast * (other[i] * axis[j] + axis[i] * other[j]) for i, j in pairs]
    for k, row in enumerate(rows):
        coef[k] = row


def chunk_sensitivities(chunk, quads, grads, coef, sens, squares, wide, diffs):
    comps, electrodes, _ = wide.shape
    readings = squares.shape[0]
    block = 256

    @pl.loop(0, electrodes // block)
    def _(i):
        at = pl.multiple_of(i * block, block)
        for c in range(comps):
            wide[c, pl.ds(at, block), :] = grads[c, pl.ds(at, block), :].astype(jnp.float32)

    @pl.loop(0, readings // 8)
    def _(g):
        for u in range(8):
            q = g * 8 + u
            a, b, m, n = (quads[j, q] for j in range(4))
            for c in range(comps):
                diffs[c, pl.ds(q, 1), :] = wide[c, pl.ds(a, 1), :] - wide[c, pl.ds(b, 1), :]
                diffs[comps + c, pl.ds(q, 1), :] = wide[c, pl.ds(m, 1), :] - wide[c, pl.ds(n, 1), :]

    tile = 16

    @pl.loop(0, readings // tile)
    def _(i):
        at = pl.multiple_of(i * tile, tile)
        s = [diffs[c, pl.ds(at, tile), :] for c in range(3)]
        r = [diffs[3 + c, pl.ds(at, tile), :] for c in range(3)]
        terms = [s[c] * r[c] for c in range(3)]
        terms += [s[i] * r[j] + s[j] * r[i] for i, j in ((0, 1), (0, 2), (1, 2))]
        square = squares[pl.ds(at, tile), :]
        for p in range(4):
            value = terms[0] * coef[6 * p, pl.ds(chunk, 1), :]
            for k in range(1, 6):
                value = value + terms[k] * coef[6 * p + k, pl.ds(chunk, 1), :]
            sens[pl.ds(4 * at + p, tile, stride=4), :] = value
            square = square + value * value
        squares[pl.ds(at, tile), :] = square


def exchange_kernel(
    n, quads, fields, horiz, vertical, sin_t, cos_t, sin_p, cos_p, sens, total,
    landed, ready, wide, diffs, squares, coef, part, slots,
    send_sem, recv_sem, own_sem, out_sem, part_send_sem, part_recv_sem,
):
    me = lax.axis_index("cell")
    rows = fields.shape[1]
    chunks = landed.shape[0]
    cells = chunks * LANES
    greet(n, me)

    def landing(chunk):
        return landed.at[chunk, :, pl.ds(pl.multiple_of(me * rows, rows), rows), :]

    def leaving(device, chunk):
        return fields.at[:, :, pl.ds(pl.multiple_of(device * cells + chunk * LANES, LANES), LANES)]

    def copy(chunk, step):
        peer = lax.rem(me + step, n)
        return pltpu.make_async_remote_copy(
            src_ref=leaving(peer, chunk),
            dst_ref=landing(chunk),
            send_sem=send_sem.at[chunk, step],
            recv_sem=recv_sem.at[chunk, step],
            device_id={"cell": peer},
            device_id_type=MESH,
        )

    def own(chunk):
        return pltpu.make_async_copy(leaving(me, chunk), landing(chunk), own_sem.at[chunk])

    def out(chunk):
        at = pl.ds(pl.multiple_of(chunk * LANES, LANES), LANES)
        return pltpu.make_async_copy(ready.at[chunk], sens.at[:, at], out_sem.at[chunk])

    @pl.loop(0, chunks)
    def _(chunk):
        own(chunk).start()

        @pl.loop(1, n)
        def _(step):
            copy(chunk, step).start()

    squares[...] = jnp.zeros_like(squares)
    fill_coefficients(coef, *(x[...] for x in (horiz, vertical, sin_t, cos_t, sin_p, cos_p)))

    @pl.loop(0, chunks)
    def _(chunk):
        own(chunk).wait()

        @pl.loop(1, n)
        def _(step):
            copy(chunk, step).wait()

        chunk_sensitivities(
            chunk, quads, landed.at[chunk], coef, ready.at[chunk], squares, wide, diffs
        )
        out(chunk).start()

    def copy_part(step):
        return pltpu.make_async_remote_copy(
            src_ref=part,
            dst_ref=slots.at[step],
            send_sem=part_send_sem.at[step],
            recv_sem=part_recv_sem.at[step],
            device_id={"cell": lax.rem(me + step, n)},
            device_id_type=MESH,
        )

    part[...] = jnp.sum(squares[...].reshape(*part.shape, LANES), axis=-1)

    @pl.loop(1, n)
    def _(step):
        copy_part(step).start()

    slots[0] = part[...]

    @pl.loop(0, chunks)
    def _(chunk):
        out(chunk).wait()

    @pl.loop(1, n)
    def _(step):
        copy_part(step).wait()

    total[...] = jnp.sum(slots[...], axis=0)


def sensitivities(fields, quads, cell_values, n):
    comps, rows, _ = fields.shape
    chunks = cell_values[0].shape[0]
    electrodes, readings, cells = rows * n, quads.shape[1], chunks * LANES
    sums = (readings // LANES, LANES)
    in_vmem = pl.BlockSpec(memory_space=pltpu.VMEM)
    anywhere = pl.BlockSpec(memory_space=pl.ANY)
    return pl.pallas_call(
        functools.partial(exchange_kernel, n),
        out_shape=[
            jax.ShapeDtypeStruct((readings * 4, cells), jnp.float32),
            jax.ShapeDtypeStruct(sums, jnp.float32),
        ],
        in_specs=[pl.BlockSpec(memory_space=pltpu.SMEM), anywhere] + [in_vmem] * len(cell_values),
        out_specs=[anywhere, in_vmem],
        scratch_shapes=[
            pltpu.VMEM((chunks, comps, electrodes, LANES), fields.dtype),
            pltpu.VMEM((chunks, readings * 4, LANES), jnp.float32),
            pltpu.VMEM((comps, electrodes, LANES), jnp.float32),
            pltpu.VMEM((2 * comps, readings, LANES), jnp.float32),
            pltpu.VMEM((readings, LANES), jnp.float32),
            pltpu.VMEM((24, chunks, LANES), jnp.float32),
            pltpu.VMEM(sums, jnp.float32),
            pltpu.VMEM((n, *sums), jnp.float32),
            pltpu.SemaphoreType.DMA((chunks, n)),
            pltpu.SemaphoreType.DMA((chunks, n)),
            pltpu.SemaphoreType.DMA((chunks,)),
            pltpu.SemaphoreType.DMA((chunks,)),
            pltpu.SemaphoreType.DMA((n,)),
            pltpu.SemaphoreType.DMA((n,)),
        ],
        compiler_params=pltpu.CompilerParams(
            collective_id=0, has_side_effects=True, vmem_limit_bytes=56 * 2**20
        ),
        name="exchange",
    )(quads, fields, *cell_values)


def norm_kernel(sens, scale, jacobian, coverage):
    count = sens.shape[0]

    @pl.when(pl.program_id(0) == 0)
    def _():
        coverage[...] = jnp.zeros_like(coverage)

    for lane in range(sens.shape[1] // LANES):
        at = pl.ds(lane * LANES, LANES)
        normed = sens[:, at] * scale[...]
        jacobian[:, :, at] = normed.reshape(count // 4, 4, LANES).astype(jnp.bfloat16)
        coverage[:, at] += jnp.sum((normed * normed).reshape(count // 8, 8, LANES), axis=0)


def normalise(sens, scale):
    rows, cells = sens.shape
    block = 1024
    return pl.pallas_call(
        norm_kernel,
        grid=(rows // block,),
        in_specs=[
            pl.BlockSpec((block, cells), lambda i: (i, 0)),
            pl.BlockSpec((block, LANES), lambda i: (i, 0)),
        ],
        out_specs=[
            pl.BlockSpec((block // 4, 4, cells), lambda i: (i, 0, 0)),
            pl.BlockSpec((8, cells), lambda i: (0, 0)),
        ],
        out_shape=[
            jax.ShapeDtypeStruct((rows // 4, 4, cells), jnp.bfloat16),
            jax.ShapeDtypeStruct((8, cells), jnp.float32),
        ],
        compiler_params=pltpu.CompilerParams(vmem_limit_bytes=48 * 2**20),
        name="norm",
    )(sens, scale)


def local(fields, horiz, vertical, tilt_angle, azimuth, electrode_quads):
    shards = lax.axis_size("cell")
    cells = horiz.shape[0]
    readings = electrode_quads.shape[0]
    values = (
        horiz, vertical, jnp.sin(tilt_angle), jnp.cos(tilt_angle), jnp.sin(azimuth), jnp.cos(azimuth)
    )
    sens, total = sensitivities(
        fields.transpose(1, 0, 2),
        electrode_quads.T,
        [x.reshape(cells // LANES, LANES) for x in values],
        shards,
    )
    meansq = total.reshape(-1) / (4.0 * cells * shards)
    scale = jnp.broadcast_to(lax.rsqrt(meansq + 1e-06)[:, None, None], (readings, 4, LANES))
    jacobian, coverage = normalise(sens, scale.reshape(readings * 4, LANES))
    return jacobian, jnp.sum(coverage, axis=0)


def solution(mesh):
    placed = (
        P(("grp", "cell"), None, None),
        P(("grp", "cell")),
        P(("grp", "cell")),
        P(("grp", "cell")),
        P(("grp", "cell")),
        P("grp", None),
    )
    return jax.shard_map(
        local,
        mesh=mesh,
        in_specs=placed,
        out_specs=(P("grp", None, "cell"), P(("grp", "cell"))),
        check_vma=False,
    )
```

```python
import functools

import jax
import jax.numpy as jnp
from jax import lax
from jax.experimental import pallas as pl
from jax.experimental.pallas import tpu as pltpu
from jax.sharding import PartitionSpec as P

MESH = pl.DeviceIdType.MESH
LANES = 128


def greet(n, me):
    barrier = pltpu.get_barrier_semaphore()

    @pl.loop(1, n)
    def _(step):
        pl.semaphore_signal(barrier, inc=1, device_id={"cell": lax.rem(me + step, n)}, device_id_type=MESH)

    pl.semaphore_wait(barrier, n - 1)


def fill_coefficients(coef, horiz, vertical, sin_t, cos_t, sin_p, cos_p):
    axis = (sin_t * cos_p, sin_t * sin_p, cos_t)
    tilt = (cos_t * cos_p, cos_t * sin_p, -sin_t)
    turn = (-sin_t * sin_p, sin_t * cos_p, jnp.zeros_like(sin_t))
    contrast = vertical - horiz
    pairs = ((0, 0), (1, 1), (2, 2), (0, 1), (0, 2), (1, 2))
    rows = [-horiz * ((1.0 if i == j else 0.0) - axis[i] * axis[j]) for i, j in pairs]
    rows += [-vertical * axis[i] * axis[j] for i, j in pairs]
    for other in (tilt, turn):
        rows += [-contrast * (other[i] * axis[j] + axis[i] * other[j]) for i, j in pairs]
    for k, row in enumerate(rows):
        coef[k] = row


def chunk_sensitivities(chunk, quads, grads, coef, sens, squares, wide, diffs):
    comps, electrodes, _ = wide.shape
    readings = squares.shape[0]
    block = 256

    @pl.loop(0, electrodes // block)
    def _(i):
        at = pl.multiple_of(i * block, block)
        for c in range(comps):
            wide[c, pl.ds(at, block), :] = grads[c, pl.ds(at, block), :].astype(jnp.float32)

    @pl.loop(0, readings // 8)
    def _(g):
        at = pl.multiple_of(g * 8, 8)
        rows = []
        for u in range(8):
            a, b, m, n = (quads[j, at + u] for j in range(4))
            rows += [wide[c, pl.ds(a, 1), :] - wide[c, pl.ds(b, 1), :] for c in range(comps)]
            rows += [wide[c, pl.ds(m, 1), :] - wide[c, pl.ds(n, 1), :] for c in range(comps)]
        for u in range(8):
            for c in range(2 * comps):
                diffs[c, pl.ds(at + u, 1), :] = rows[2 * comps * u + c]

    tile = 16

    @pl.loop(0, readings // tile)
    def _(i):
        at = pl.multiple_of(i * tile, tile)
        s = [diffs[c, pl.ds(at, tile), :] for c in range(3)]
        r = [diffs[3 + c, pl.ds(at, tile), :] for c in range(3)]
        terms = [s[c] * r[c] for c in range(3)]
        terms += [s[i] * r[j] + s[j] * r[i] for i, j in ((0, 1), (0, 2), (1, 2))]
        square = squares[pl.ds(at, tile), :]
        for p in range(4):
            value = terms[0] * coef[6 * p, pl.ds(chunk, 1), :]
            for k in range(1, 6):
                value = value + terms[k] * coef[6 * p + k, pl.ds(chunk, 1), :]
            sens[pl.ds(4 * at + p, tile, stride=4), :] = value
            square = square + value * value
        squares[pl.ds(at, tile), :] = square


def exchange_kernel(
    n, quads, fields, horiz, vertical, sin_t, cos_t, sin_p, cos_p, sens, total,
    landed, ready, wide, diffs, squares, coef, part, slots,
    send_sem, recv_sem, own_sem, out_sem, part_send_sem, part_recv_sem,
):
    me = lax.axis_index("cell")
    rows = fields.shape[1]
    chunks = landed.shape[0]
    cells = chunks * LANES
    greet(n, me)

    def landing(chunk):
        return landed.at[chunk, :, pl.ds(pl.multiple_of(me * rows, rows), rows), :]

    def leaving(device, chunk):
        return fields.at[:, :, pl.ds(pl.multiple_of(device * cells + chunk * LANES, LANES), LANES)]

    def copy(chunk, step):
        peer = lax.rem(me + step, n)
        return pltpu.make_async_remote_copy(
            src_ref=leaving(peer, chunk),
            dst_ref=landing(chunk),
            send_sem=send_sem.at[chunk, step],
            recv_sem=recv_sem.at[chunk, step],
            device_id={"cell": peer},
            device_id_type=MESH,
        )

    def own(chunk):
        return pltpu.make_async_copy(leaving(me, chunk), landing(chunk), own_sem.at[chunk])

    def out(chunk):
        at = pl.ds(pl.multiple_of(chunk * LANES, LANES), LANES)
        return pltpu.make_async_copy(ready.at[chunk], sens.at[:, at], out_sem.at[chunk])

    @pl.loop(0, chunks)
    def _(chunk):
        own(chunk).start()

        @pl.loop(1, n)
        def _(step):
            copy(chunk, step).start()

    squares[...] = jnp.zeros_like(squares)
    fill_coefficients(coef, *(x[...] for x in (horiz, vertical, sin_t, cos_t, sin_p, cos_p)))

    @pl.loop(0, chunks)
    def _(chunk):
        own(chunk).wait()

        @pl.loop(1, n)
        def _(step):
            copy(chunk, step).wait()

        chunk_sensitivities(
            chunk, quads, landed.at[chunk], coef, ready.at[chunk], squares, wide, diffs
        )
        out(chunk).start()

    def copy_part(step):
        return pltpu.make_async_remote_copy(
            src_ref=part,
            dst_ref=slots.at[step],
            send_sem=part_send_sem.at[step],
            recv_sem=part_recv_sem.at[step],
            device_id={"cell": lax.rem(me + step, n)},
            device_id_type=MESH,
        )

    part[...] = jnp.sum(squares[...].reshape(*part.shape, LANES), axis=-1)

    @pl.loop(1, n)
    def _(step):
        copy_part(step).start()

    slots[0] = part[...]

    @pl.loop(0, chunks)
    def _(chunk):
        out(chunk).wait()

    @pl.loop(1, n)
    def _(step):
        copy_part(step).wait()

    total[...] = jnp.sum(slots[...], axis=0)


def sensitivities(fields, quads, cell_values, n):
    comps, rows, _ = fields.shape
    chunks = cell_values[0].shape[0]
    electrodes, readings, cells = rows * n, quads.shape[1], chunks * LANES
    sums = (readings // LANES, LANES)
    in_vmem = pl.BlockSpec(memory_space=pltpu.VMEM)
    anywhere = pl.BlockSpec(memory_space=pl.ANY)
    return pl.pallas_call(
        functools.partial(exchange_kernel, n),
        out_shape=[
            jax.ShapeDtypeStruct((readings * 4, cells), jnp.float32),
            jax.ShapeDtypeStruct(sums, jnp.float32),
        ],
        in_specs=[pl.BlockSpec(memory_space=pltpu.SMEM), anywhere] + [in_vmem] * len(cell_values),
        out_specs=[anywhere, in_vmem],
        scratch_shapes=[
            pltpu.VMEM((chunks, comps, electrodes, LANES), fields.dtype),
            pltpu.VMEM((chunks, readings * 4, LANES), jnp.float32),
            pltpu.VMEM((comps, electrodes, LANES), jnp.float32),
            pltpu.VMEM((2 * comps, readings, LANES), jnp.float32),
            pltpu.VMEM((readings, LANES), jnp.float32),
            pltpu.VMEM((24, chunks, LANES), jnp.float32),
            pltpu.VMEM(sums, jnp.float32),
            pltpu.VMEM((n, *sums), jnp.float32),
            pltpu.SemaphoreType.DMA((chunks, n)),
            pltpu.SemaphoreType.DMA((chunks, n)),
            pltpu.SemaphoreType.DMA((chunks,)),
            pltpu.SemaphoreType.DMA((chunks,)),
            pltpu.SemaphoreType.DMA((n,)),
            pltpu.SemaphoreType.DMA((n,)),
        ],
        compiler_params=pltpu.CompilerParams(
            collective_id=0, has_side_effects=True, vmem_limit_bytes=56 * 2**20
        ),
        name="exchange",
    )(quads, fields, *cell_values)


def norm_kernel(sens, scale, jacobian, coverage):
    count = sens.shape[0]

    @pl.when(pl.program_id(0) == 0)
    def _():
        coverage[...] = jnp.zeros_like(coverage)

    for lane in range(sens.shape[1] // LANES):
        at = pl.ds(lane * LANES, LANES)
        normed = sens[:, at] * scale[...]
        jacobian[:, :, at] = normed.reshape(count // 4, 4, LANES).astype(jnp.bfloat16)
        coverage[:, at] += jnp.sum((normed * normed).reshape(count // 8, 8, LANES), axis=0)


def normalise(sens, scale):
    rows, cells = sens.shape
    block = 1024
    return pl.pallas_call(
        norm_kernel,
        grid=(rows // block,),
        in_specs=[
            pl.BlockSpec((block, cells), lambda i: (i, 0)),
            pl.BlockSpec((block, LANES), lambda i: (i, 0)),
        ],
        out_specs=[
            pl.BlockSpec((block // 4, 4, cells), lambda i: (i, 0, 0)),
            pl.BlockSpec((8, cells), lambda i: (0, 0)),
        ],
        out_shape=[
            jax.ShapeDtypeStruct((rows // 4, 4, cells), jnp.bfloat16),
            jax.ShapeDtypeStruct((8, cells), jnp.float32),
        ],
        compiler_params=pltpu.CompilerParams(vmem_limit_bytes=48 * 2**20),
        name="norm",
    )(sens, scale)


def local(fields, horiz, vertical, tilt_angle, azimuth, electrode_quads):
    shards = lax.axis_size("cell")
    cells = horiz.shape[0]
    readings = electrode_quads.shape[0]
    values = (
        horiz, vertical, jnp.sin(tilt_angle), jnp.cos(tilt_angle), jnp.sin(azimuth), jnp.cos(azimuth)
    )
    sens, total = sensitivities(
        fields.transpose(1, 0, 2),
        electrode_quads.T,
        [x.reshape(cells // LANES, LANES) for x in values],
        shards,
    )
    meansq = total.reshape(-1) / (4.0 * cells * shards)
    scale = jnp.broadcast_to(lax.rsqrt(meansq + 1e-06)[:, None, None], (readings, 4, LANES))
    jacobian, coverage = normalise(sens, scale.reshape(readings * 4, LANES))
    return jacobian, jnp.sum(coverage, axis=0)


def solution(mesh):
    placed = (
        P(("grp", "cell"), None, None),
        P(("grp", "cell")),
        P(("grp", "cell")),
        P(("grp", "cell")),
        P(("grp", "cell")),
        P("grp", None),
    )
    return jax.shard_map(
        local,
        mesh=mesh,
        in_specs=placed,
        out_specs=(P("grp", None, "cell"), P(("grp", "cell"))),
        check_vma=False,
    )
```
